32 devices in a mesh: groups: 2 (over y), col: 4 (over z), row: 4 (over x, core).
Axes of the slice: x: 2, y: 2, z: 4, core: 2. Of those that a mesh axis runs over, the one named last changes fastest.
Arguments:
- diag_block: float32 [256, 256], P('row', 'col'), as said below
- panel_low: float32 [16384, 256], P(('groups', 'row'), 'col'), parts along dimension 0, may hold values from -1.5 to 1.5
- slab_rows: float32 [512, 16384], P('col', ('groups', 'row')), parts along dimension 1, may hold values from -6 to 6
- rhs_top: float32 [512, 256], P(('groups', 'col'), 'row'), parts along dimension 0, may hold values from -6 to 6
- rhs_low: float32 [256, 16384], P('col', ('groups', 'row')), parts along dimension 1, may hold values from -6 to 6
Outputs:
- panel_factor: float32 [16384, 256], P(('groups', 'row'), 'col'), parts along dimension 0
- slab_update: float32 [512, 16384], P('col', ('groups', 'row')), parts along dimension 1
- rhs_solved: float32 [512, 256], P(('groups', 'col'), 'row'), parts along dimension 0
- rhs_update: float32 [256, 16384], P('col', ('groups', 'row')), parts along dimension 1
The draws below stay inside these ranges and needn't reach their ends.
There are 2 independent parts, one for each index of `groups`. The reference program is written for one: setup_inputs(seed, part) draws one part's arguments, and reference() takes and returns one part's arrays. A program takes and returns all parts, laid end to end along the dimension named above; an argument that names none is the same for every part. Nothing has to cross between parts.
Inputs may be any that keep to these rules, and one draw needn't show every extreme that they name: diag_block is symmetric and positive definite, the sum of a positive definite kernel matrix and a positive diagonal.
All inputs are finite; a program needn't handle non-finite values.
Results may differ from the reference program's by a relative error of at most 0.00015.
Values sent between devices are 32-bit elements; how exact they have to be, the bound alone decides.
A program may use at most 64 MiB of HBM per device.

```python
import jax
import jax.numpy as jnp
from jax import lax

NB = 256
SLAB = 512
NRHS = 256
MR = 8192


def draw_diag_block(key, part):
    key_scale = jax.random.fold_in(key, 11)
    key_noise = jax.random.fold_in(key, 12)
    key_place = jax.random.fold_in(key, 13)
    scales = jnp.exp(jax.random.uniform(key_scale, (NB,), jnp.float32, jnp.log(0.7), jnp.log(1.4)))
    reach = 0.5
    noise = jax.random.uniform(key_noise, (NB,), jnp.float32, 0.5, 1.5)
    places = jax.random.uniform(key_place, (NB, 3), jnp.float32, 0.0, 1.0)
    gap_first = places[:, 0][:, None] - places[:, 0][None, :]
    gap_second = places[:, 1][:, None] - places[:, 1][None, :]
    gap_third = places[:, 2][:, None] - places[:, 2][None, :]
    distance = jnp.sqrt(gap_first * gap_first + gap_second * gap_second + gap_third * gap_third)
    kernel = scales[:, None] * scales[None, :] * jnp.exp(-distance / reach)
    return (kernel + jnp.diag(noise)).astype(jnp.float32)


def block_levels(key, dims, split, low, high):
    gain = 1.0
    for dim, parts in split:
        heights = jax.random.uniform(jax.random.fold_in(jax.random.fold_in(key, 6), dim), (parts,), jnp.float32, low / len(split), high / len(split))
        gain = gain * jnp.repeat(jnp.exp(heights), dims[dim] // parts).reshape((-1,) + (1,) * (len(dims) - 1 - dim))
    return gain


def centred(stream_key, extent, spread, most, split=(), dtype=jnp.bfloat16):
    array = jax.random.normal(stream_key, extent, jnp.float32) * spread
    if len(split) > 0:
        array = block_levels(stream_key, extent, split, -0.22, 0.18) * array
    return jnp.clip(array, min=-most, max=most).astype(dtype)


def setup_inputs(seed: int = 0, part: int = 0) -> dict:
    splits = jax.random.split(jax.random.key(seed), 6)
    part_splits = jax.random.split(jax.random.fold_in(splits[5], part), 6)
    return {
        "diag_block": draw_diag_block(jax.random.fold_in(splits[5], 71), part),
        "panel_low": centred(part_splits[1], (MR, NB), 0.25, 1.5, ((0, 4), (1, 4)), jnp.float32),
        "slab_rows": centred(part_splits[2], (SLAB, MR), 1.0, 6.0, ((0, 4), (1, 4)), jnp.float32),
        "rhs_top": centred(part_splits[3], (NRHS, NB), 1.0, 6.0, ((0, 4), (1, 4)), jnp.float32),
        "rhs_low": centred(part_splits[4], (NRHS, MR), 1.0, 6.0, ((0, 4), (1, 4)), jnp.float32),
    }


def solve_right(factor, rows):
    return jax.scipy.linalg.solve_triangular(factor, rows.T, lower=True).T

def reference(diag_block, panel_low, slab_rows, rhs_top, rhs_low):
    factor = jnp.linalg.cholesky(diag_block)
    panel_factor = solve_right(factor, panel_low)
    rhs_solved = solve_right(factor, rhs_top)
    slab_update = slab_rows - jnp.dot(panel_factor[:SLAB].astype(jnp.float32), panel_factor.T.astype(jnp.float32), precision=lax.Precision.HIGHEST, preferred_element_type=jnp.float32)
    rhs_update = rhs_low - jnp.dot(rhs_solved.astype(jnp.float32), panel_factor.T.astype(jnp.float32), precision=lax.Precision.HIGHEST, preferred_element_type=jnp.float32)
    return (panel_factor, slab_update, rhs_solved, rhs_update)
```

```python
import functools

import jax
import jax.numpy as jnp
from jax import lax
from jax.experimental import pallas as pl
from jax.experimental.pallas import tpu as pltpu
from jax.sharding import PartitionSpec as P

MESH = pl.DeviceIdType.MESH
BS = 64
CHUNKS = 4
HIGH = lax.Precision.HIGHEST


def dot(a, b, contract=((1,), (0,))):
    return lax.dot_general(
        a, b, (contract, ((), ())), precision=HIGH, preferred_element_type=jnp.float32
    )


def eliminate(block, between):
    row = lax.broadcasted_iota(jnp.int32, (BS, 2 * BS), 0)
    lane = lax.broadcasted_iota(jnp.int32, (BS, 2 * BS), 1)
    eye = jnp.where(row[:, :BS] == lane[:, :BS], 1.0, 0.0).astype(jnp.float32)
    y = jnp.concatenate([block, eye], axis=1)
    groups = [y[g * 8 : g * 8 + 8] for g in range(BS // 8)]
    sub = row[:8]
    for k in range(BS):
        if k % 16 == 0:
            between(k // 16)
        g0, s0 = k // 8, k % 8
        pivot_row = groups[g0][s0 : s0 + 1, :]
        d = pivot_row[:, k : k + 1]
        scale = lax.rsqrt(d)
        r = pivot_row * scale
        col = groups[g0][:, k : k + 1] * scale
        groups[g0] = jnp.where(
            sub == s0,
            jnp.broadcast_to(r, (8, 2 * BS)),
            groups[g0] - jnp.where(sub > s0, col, 0.0) * r,
        )
        for g in range(g0 + 1, BS // 8):
            groups[g] = groups[g] - (groups[g][:, k : k + 1] * scale) * r
    return jnp.concatenate(groups, axis=0)[:, BS:]


def gather_kernel(
    ncol, nrow, pack, slab_count,
    diag_ref, panel_ref, rhs_ref,
    pt_ref, lr_ref, rs_ref,
    dpack, dslots, raw, left, rslots, aug, linv,
    dsend, drecv, rsend, rrecv, l1send, l1recv, l2send, l2recv, usend, wsend, precv,
):
    mc = lax.axis_index("col")
    mr = lax.axis_index("row")
    n = ncol * nrow
    me = mc * nrow + mr
    dr, dc = diag_ref.shape
    rows, w = panel_ref.shape
    nb = w * ncol
    chunk = rows // CHUNKS
    rk = rhs_ref.shape[1]

    def peer(t):
        p = lax.rem(me + t, n)
        return p // nrow, lax.rem(p, nrow), p

    barrier = pltpu.get_barrier_semaphore()

    def greet(t, carry):
        pc, pr, _ = peer(t)
        pl.semaphore_signal(barrier, inc=1, device_id={"col": pc, "row": pr}, device_id_type=MESH)
        return carry

    lax.fori_loop(1, n, greet, 0)

    x = diag_ref[...]
    step = dr // pack
    dpack[...] = jnp.concatenate([x[i * step : (i + 1) * step] for i in range(pack)], axis=1)
    dslots[me] = dpack[...]
    rslots[mr] = rhs_ref[...]
    mine = pl.ds(pl.multiple_of(mc * w, w), w)
    raw[mine, :] = panel_ref[...].T
    root = (mc * slab_count) // rows

    pl.semaphore_wait(barrier, n - 1)

    def diag_copy(t):
        pc, pr, p = peer(t)
        return pltpu.make_async_remote_copy(
            dpack, dslots.at[me], dsend.at[t], drecv.at[me],
            device_id={"col": pc, "row": pr}, device_id_type=MESH,
        )

    def diag_wait(p):
        return pltpu.make_async_remote_copy(
            dpack, dslots.at[p], dsend.at[0], drecv.at[p],
            device_id={"col": mc, "row": mr}, device_id_type=MESH,
        )

    def rhs_copy(t, slot):
        return pltpu.make_async_remote_copy(
            rhs_ref, rslots.at[slot], rsend.at[t], rrecv.at[slot],
            device_id={"col": mc, "row": lax.rem(mr + t, nrow)}, device_id_type=MESH,
        )

    def left_piece(t, k):
        c = lax.rem(mc + t, ncol)
        off = pl.multiple_of(lax.rem(c * slab_count, rows), slab_count)
        at = pl.ds(pl.multiple_of(k * w, w), w)
        return pltpu.make_async_remote_copy(
            raw.at[mine, pl.ds(off, slab_count)], left.at[at, :],
            l1send.at[t], l1recv.at[k],
            device_id={"col": c, "row": mr}, device_id_type=MESH,
        )

    def left_whole(t):
        return pltpu.make_async_remote_copy(
            left, left, l2send.at[t], l2recv,
            device_id={"col": mc, "row": lax.rem(mr + t, nrow)}, device_id_type=MESH,
        )

    def piece(block, q, sends, to):
        part = raw.at[
            pl.ds(pl.multiple_of(block * w, w), w),
            pl.ds(pl.multiple_of(q * chunk, chunk), chunk),
        ]
        return pltpu.make_async_remote_copy(
            part, part, sends.at[block, q], precv.at[block, q],
            device_id={"col": to, "row": mr}, device_id_type=MESH,
        )

    def loop(lo, hi, body):
        def run(i, carry):
            body(i)
            return carry

        lax.fori_loop(lo, hi, run, 0)

    loop(1, n, lambda t: diag_copy(t).start())

    def left_root(t):
        return ((lax.rem(mc + t, ncol)) * slab_count) // rows == mr

    def send_left(t):
        @pl.when(left_root(t))
        def _():
            left_piece(t, mc).start()

    loop(1, ncol, send_left)

    @pl.when(root == mr)
    def _():
        off = pl.multiple_of(lax.rem(mc * slab_count, rows), slab_count)
        left[mine, :] = raw[mine, pl.ds(off, slab_count)]

    loop(1, nrow, lambda t: rhs_copy(t, mr).start())

    def send_own(q):
        @pl.when(mc + 1 < ncol)
        def _():
            piece(mc, q, usend, mc + 1).start()

        @pl.when(mc > 0)
        def _():
            piece(mc, q, wsend, mc - 1).start()

    loop(0, CHUNKS, send_own)

    events = (ncol - 1) * CHUNKS
    points = (nb // BS) * (BS // 16)
    each = -(-events // points)

    def forward(e):
        s = e // CHUNKS + 1
        q = lax.rem(e, CHUNKS)

        @pl.when(jnp.logical_and(mc - s >= 0, mc + 1 < ncol))
        def _():
            piece(mc - s, q, usend, mc + 1).wait_recv()
            piece(mc - s, q, usend, mc + 1).start()

        @pl.when(jnp.logical_and(mc + s < ncol, mc > 0))
        def _():
            piece(mc + s, q, wsend, mc - 1).wait_recv()
            piece(mc + s, q, wsend, mc - 1).start()

    loop(1, n, lambda t: diag_wait(peer(t)[2]).wait_recv())

    for r in range(nrow):
        parts = []
        for c in range(ncol):
            v = dslots[c * nrow + r]
            parts.append(
                jnp.concatenate([v[:, i * dc : (i + 1) * dc] for i in range(pack)], axis=0)
            )
        aug[r * dr : (r + 1) * dr, :nb] = jnp.concatenate(parts, axis=1)
    ri = lax.broadcasted_iota(jnp.int32, (nb, nb), 0)
    ci = lax.broadcasted_iota(jnp.int32, (nb, nb), 1)
    aug[:, nb:] = jnp.where(ri == ci, 1.0, 0.0).astype(jnp.float32)

    def block_step(b):
        @pl.when(jnp.logical_and(b == 1, root == mr))
        def _():
            def wait_piece(t):
                left_piece(t, lax.rem(mc + t, ncol)).wait_recv()

            loop(1, ncol, wait_piece)
            loop(1, nrow, lambda t: left_whole(t).start())

        here = pl.ds(pl.multiple_of(b * BS, BS), BS)
        panel = aug[here, :]
        rolled = pltpu.roll(panel[:, :nb], lax.rem(nb - b * BS, nb), 1)

        def between(i):
            point = b * (BS // 16) + i
            loop(
                jnp.minimum(point * each, events),
                jnp.minimum((point + 1) * each, events),
                forward,
            )

        winv = eliminate(rolled[:, :BS], between)
        upper = dot(winv, panel)
        linv[here, :] = upper[:, nb:]
        lane = lax.broadcasted_iota(jnp.int32, (BS, nb), 1)
        later = jnp.where(lane >= (b + 1) * BS, upper[:, :nb], 0.0)
        aug[...] = aug[...] - dot(later, upper, ((0,), (0,)))

    loop(0, nb // BS, block_step)

    @pl.when(root != mr)
    def _():
        left_whole(0).wait_recv()

    loop(1, nrow, lambda t: rhs_copy(t, lax.rem(mr + t, nrow)).wait_recv())
    inv = linv[...]
    top = jnp.concatenate([rslots[r].T for r in range(nrow)], axis=0)
    left_t = dot(inv, left[...])
    top_t = dot(inv, top)
    lr_ref[:slab_count, :] = left_t.T
    rt = top_t.T
    lr_ref[slab_count:, :] = rt
    picked = pltpu.roll(rt, lax.rem(nb - mr * rk, nb), 1)
    rs_ref[...] = picked[:, :rk]

    def finish(q):
        def arrived(t):
            block = lax.rem(mc + t, ncol)

            @pl.when(jnp.logical_or(
                jnp.logical_and(block < mc, mc + 1 >= ncol),
                jnp.logical_and(block > mc, mc <= 0),
            ))
            def _():
                piece(block, q, usend, mc).wait_recv()

        loop(1, ncol, arrived)
        at = pl.ds(pl.multiple_of(q * chunk, chunk), chunk)
        pt_ref[:, at] = dot(linv[...], raw[:, at])

    loop(0, CHUNKS, finish)

    loop(1, n, lambda t: diag_copy(t).wait_send())
    loop(1, nrow, lambda t: rhs_copy(t, mr).wait_send())

    def sent_left(t):
        @pl.when(left_root(t))
        def _():
            left_piece(t, mc).wait_send()

    loop(1, ncol, sent_left)

    @pl.when(root == mr)
    def _():
        loop(1, nrow, lambda t: left_whole(t).wait_send())

    def sent(block):
        def chunk_sent(q):
            @pl.when(jnp.logical_and(block <= mc, mc + 1 < ncol))
            def _():
                piece(block, q, usend, mc + 1).wait_send()

            @pl.when(jnp.logical_and(block >= mc, mc > 0))
            def _():
                piece(block, q, wsend, mc - 1).wait_send()

        loop(0, CHUNKS, chunk_sent)

    loop(0, ncol, sent)


def update_kernel(w, slab_count, pt_ref, lr_ref, rs_ref, slab_ref, low_ref,
                  pf_ref, su_ref, rso_ref, ru_ref):
    mc = lax.axis_index("col")
    prod = dot(lr_ref[...], pt_ref[...])
    su_ref[...] = slab_ref[...] - prod[:slab_count]
    ru_ref[...] = low_ref[...] - prod[slab_count:]
    pf_ref[...] = pt_ref[pl.ds(pl.multiple_of(mc * w, w), w), :].T
    rso_ref[...] = rs_ref[...]


def local(ncol, nrow, diag_block, panel_low, slab_rows, rhs_top, rhs_low):
    dr, dc = diag_block.shape
    rows, w = panel_low.shape
    nb = w * ncol
    slab_count = slab_rows.shape[0]
    nrhs, rk = rhs_top.shape
    pack = 128 // dc
    if dr % (8 * pack):
        pack = 1
    n = ncol * nrow
    f32 = jnp.float32
    vm = pl.BlockSpec(memory_space=pltpu.VMEM)
    dma = pltpu.SemaphoreType.DMA
    pt, lr, rs = pl.pallas_call(
        functools.partial(gather_kernel, ncol, nrow, pack, slab_count),
        out_shape=(
            jax.ShapeDtypeStruct((nb, rows), f32),
            jax.ShapeDtypeStruct((slab_count + nrhs, nb), f32),
            jax.ShapeDtypeStruct((nrhs, rk), f32),
        ),
        in_specs=[vm] * 3,
        out_specs=(vm,) * 3,
        scratch_shapes=[
            pltpu.VMEM((dr // pack, dc * pack), f32),
            pltpu.VMEM((n, dr // pack, dc * pack), f32),
            pltpu.VMEM((nb, rows), f32),
            pltpu.VMEM((nb, slab_count), f32),
            pltpu.VMEM((nrow, nrhs, rk), f32),
            pltpu.VMEM((nb, 2 * nb), f32),
            pltpu.VMEM((nb, nb), f32),
            dma((n,)), dma((n,)),
            dma((nrow,)), dma((nrow,)),
            dma((ncol,)), dma((ncol,)),
            dma((nrow,)), dma,
            dma((ncol, CHUNKS)), dma((ncol, CHUNKS)), dma((ncol, CHUNKS)),
        ],
        compiler_params=pltpu.CompilerParams(
            collective_id=0, has_side_effects=True, vmem_limit_bytes=40 * 1024 * 1024
        ),
    )(diag_block, panel_low, rhs_top)
    tile = rows // 4
    return pl.pallas_call(
        functools.partial(update_kernel, w, slab_count),
        grid=(4,),
        out_shape=(
            jax.ShapeDtypeStruct((rows, w), f32),
            jax.ShapeDtypeStruct(slab_rows.shape, f32),
            jax.ShapeDtypeStruct((nrhs, rk), f32),
            jax.ShapeDtypeStruct(rhs_low.shape, f32),
        ),
        in_specs=[
            pl.BlockSpec((nb, tile), lambda i: (0, i)),
            pl.BlockSpec((slab_count + nrhs, nb), lambda i: (0, 0)),
            pl.BlockSpec((nrhs, rk), lambda i: (0, 0)),
            pl.BlockSpec((slab_count, tile), lambda i: (0, i)),
            pl.BlockSpec((nrhs, tile), lambda i: (0, i)),
        ],
        out_specs=(
            pl.BlockSpec((tile, w), lambda i: (i, 0)),
            pl.BlockSpec((slab_count, tile), lambda i: (0, i)),
            pl.BlockSpec((nrhs, rk), lambda i: (0, 0)),
            pl.BlockSpec((nrhs, tile), lambda i: (0, i)),
        ),
        compiler_params=pltpu.CompilerParams(vmem_limit_bytes=32 * 1024 * 1024),
    )(pt, lr, rs, slab_rows, rhs_low)


def solution(mesh):
    ncol, nrow = mesh.shape["col"], mesh.shape["row"]
    return jax.shard_map(
        functools.partial(local, ncol, nrow),
        mesh=mesh,
        in_specs=(
            P("row", "col"),
            P(("groups", "row"), "col"),
            P("col", ("groups", "row")),
            P(("groups", "col"), "row"),
            P("col", ("groups", "row")),
        ),
        out_specs=(
            P(("groups", "row"), "col"),
            P("col", ("groups", "row")),
            P(("groups", "col"), "row"),
            P("col", ("groups", "row")),
        ),
        check_vma=False,
    )
```

```python
import functools

import jax
import jax.numpy as jnp
from jax import lax
from jax.experimental import pallas as pl
from jax.experimental.pallas import tpu as pltpu
from jax.sharding import PartitionSpec as P

MESH = pl.DeviceIdType.MESH
BS = 64
CHUNKS = 4
PIVOTS = 8
HIGH = lax.Precision.HIGHEST


def dot(a, b, contract=((1,), (0,))):
    return lax.dot_general(
        a, b, (contract, ((), ())), precision=HIGH, preferred_element_type=jnp.float32
    )


def eliminate(block):
    shape = (8, 2 * BS)
    row = lax.broadcasted_iota(jnp.int32, (BS, BS), 0)
    lane = lax.broadcasted_iota(jnp.int32, (BS, BS), 1)
    eye = jnp.where(row == lane, 1.0, 0.0).astype(jnp.float32)
    y = jnp.concatenate([block, eye], axis=1)
    groups = [y[g * 8 : g * 8 + 8] for g in range(BS // 8)]
    sub = lax.broadcasted_iota(jnp.int32, shape, 0)

    def wide(v):
        return jnp.broadcast_to(v, shape)

    for k in range(0, BS, PIVOTS):
        g0, s0 = k // 8, k % 8
        cols = [
            {g: wide(groups[g][:, k + j : k + j + 1]) for g in range(g0, BS // 8)}
            for j in range(PIVOTS)
        ]
        rows = [wide(groups[g0][s0 + j : s0 + j + 1, :]) for j in range(PIVOTS)]
        d = [
            [wide(cols[j][g0][s0 + i : s0 + i + 1, :]) for j in range(i + 1)]
            for i in range(PIVOTS)
        ]
        for j in range(PIVOTS):
            scale = lax.rsqrt(d[j][j])
            for i in range(j + 1, PIVOTS):
                d[i][j] = d[i][j] * scale
            for i in range(j + 1, PIVOTS):
                for m in range(j + 1, i + 1):
                    d[i][m] = d[i][m] - d[i][j] * d[m][j]
            rows[j] = rows[j] * scale
            for i in range(j + 1, PIVOTS):
                rows[i] = rows[i] - d[i][j] * rows[j]
            for g in cols[j]:
                cols[j][g] = cols[j][g] * scale
                for i in range(j + 1, PIVOTS):
                    cols[i][g] = cols[i][g] - cols[j][g] * d[i][j]
        for g in range(g0, BS // 8):
            if g == g0 and s0 + PIVOTS == 8:
                new = groups[g]
            else:
                new = groups[g]
                for j in range(PIVOTS):
                    new = new - cols[j][g] * rows[j]
            if g == g0:
                new = jnp.where(sub < s0, groups[g], new)
                for j in range(PIVOTS):
                    new = jnp.where(sub == s0 + j, rows[j], new)
            groups[g] = new
    return jnp.concatenate(groups, axis=0)[:, BS:]


def gather_kernel(
    ncol, nrow, pack, slab_count,
    diag_ref, panel_ref, rhs_ref,
    pt_ref, lr_ref, rs_ref,
    dmine, dslots, raw, left, rslots, aug, linv,
    local_sem, d1send, d1recv, d2send, d2recv, rsend, rrecv,
    lsend, lrecv, usend, wsend, precv,
):
    mc = lax.axis_index("col")
    mr = lax.axis_index("row")
    dr, dc = diag_ref.shape
    w, rows = panel_ref.shape
    nb = w * ncol
    chunk = rows // CHUNKS
    rk = rhs_ref.shape[1]

    def loop(lo, hi, body):
        def run(i, carry):
            body(i)
            return carry

        lax.fori_loop(lo, hi, run, 0)

    def on_col(t):
        return {"col": lax.rem(mc + t, ncol), "row": mr}

    def on_row(t):
        return {"col": mc, "row": lax.rem(mr + t, nrow)}

    def remote(src, dst, send, recv, to):
        return pltpu.make_async_remote_copy(
            src, dst, send, recv, device_id=to, device_id_type=MESH
        )

    barrier = pltpu.get_barrier_semaphore()
    loop(1, ncol, lambda t: pl.semaphore_signal(
        barrier, inc=1, device_id=on_col(t), device_id_type=MESH))
    loop(1, nrow, lambda t: pl.semaphore_signal(
        barrier, inc=1, device_id=on_row(t), device_id_type=MESH))

    mine = pl.ds(pl.multiple_of(mc * w, w), w)
    loads = (
        pltpu.make_async_copy(diag_ref, dmine, local_sem.at[0]),
        pltpu.make_async_copy(panel_ref, raw.at[mine, :], local_sem.at[1]),
        pltpu.make_async_copy(rhs_ref, rslots.at[mr], local_sem.at[2]),
    )
    for load in loads:
        load.start()
    loads[0].wait()
    x = dmine[...]
    step = dr // pack
    dslots[mr, mc] = jnp.concatenate([x[i * step : (i + 1) * step] for i in range(pack)], axis=1)
    loads[1].wait()
    loads[2].wait()
    slab_first = mc * slab_count
    root = slab_first // rows
    slab_off = pl.multiple_of(lax.rem(slab_first, rows), slab_count)

    pl.semaphore_wait(barrier, ncol + nrow - 2)

    def diag_col(t, slot):
        at = dslots.at[mr, slot]
        return remote(at, at, d1send.at[t], d1recv.at[slot], on_col(t))

    def diag_row(t, slot):
        at = dslots.at[slot]
        return remote(at, at, d2send.at[t], d2recv.at[slot], on_row(t))

    def rhs_copy(t, slot):
        at = rslots.at[slot]
        return remote(at, at, rsend.at[t], rrecv.at[slot], on_row(t))

    def left_copy(t):
        return remote(left, left, lsend.at[t], lrecv, on_row(t))

    def piece(block, q, sends, to):
        part = raw.at[
            pl.ds(pl.multiple_of(block * w, w), w),
            pl.ds(pl.multiple_of(q * chunk, chunk), chunk),
        ]
        return remote(part, part, sends.at[block, q], precv.at[block, q], {"col": to, "row": mr})

    loop(1, ncol, lambda t: diag_col(t, mc).start())

    def send_own(q):
        @pl.when(mc + 1 < ncol)
        def _():
            piece(mc, q, usend, mc + 1).start()

        @pl.when(mc > 0)
        def _():
            piece(mc, q, wsend, mc - 1).start()

    loop(0, CHUNKS, send_own)

    loop(1, ncol, lambda t: diag_col(t, lax.rem(mc + t, ncol)).wait_recv())
    loop(1, nrow, lambda t: diag_row(t, mr).start())
    loop(1, nrow, lambda t: rhs_copy(t, mr).start())

    def forward(e):
        s = e // CHUNKS + 1
        q = lax.rem(e, CHUNKS)

        @pl.when(jnp.logical_and(mc - s >= 0, mc + 1 < ncol))
        def _():
            piece(mc - s, q, usend, mc + 1).wait_recv()
            piece(mc - s, q, usend, mc + 1).start()

        @pl.when(jnp.logical_and(mc + s < ncol, mc > 0))
        def _():
            piece(mc + s, q, wsend, mc - 1).wait_recv()
            piece(mc + s, q, wsend, mc - 1).start()

    events = max(ncol - 2, 0) * CHUNKS
    early = events // 2
    each = -(-early // (nb // BS))

    ri = lax.broadcasted_iota(jnp.int32, (nb, nb), 0)
    ci = lax.broadcasted_iota(jnp.int32, (nb, nb), 1)
    aug[:, nb:] = jnp.where(ri == ci, 1.0, 0.0).astype(jnp.float32)
    loop(1, nrow, lambda t: diag_row(t, lax.rem(mr + t, nrow)).wait_recv())
    for r in range(nrow):
        parts = []
        for c in range(ncol):
            v = dslots[r, c]
            parts.append(
                jnp.concatenate([v[:, i * dc : (i + 1) * dc] for i in range(pack)], axis=0)
            )
        aug[r * dr : (r + 1) * dr, :nb] = jnp.concatenate(parts, axis=1)

    def block_step(b):
        loop(jnp.minimum(b * each, early), jnp.minimum((b + 1) * each, early), forward)
        here = pl.ds(pl.multiple_of(b * BS, BS), BS)
        panel = aug[here, :]
        rolled = pltpu.roll(panel[:, :nb], lax.rem(nb - b * BS, nb), 1)
        winv = eliminate(rolled[:, :BS])
        upper = dot(winv, panel)
        linv[here, :] = upper[:, nb:]

        @pl.when(b + 1 < nb // BS)
        def _():
            lane = lax.broadcasted_iota(jnp.int32, (BS, nb), 1)
            later = jnp.where(lane >= (b + 1) * BS, upper[:, :nb], 0.0)
            aug[...] = aug[...] - dot(later, upper, ((0,), (0,)))

    loop(0, nb // BS, block_step)
    loop(early, events, forward)

    loop(1, nrow, lambda t: rhs_copy(t, lax.rem(mr + t, nrow)).wait_recv())
    top = jnp.concatenate([rslots[r].T for r in range(nrow)], axis=0)
    rt = dot(linv[...], top).T
    lr_ref[slab_count:, :] = rt
    rs_ref[...] = pltpu.roll(rt, lax.rem(nb - mr * rk, nb), 1)[:, :rk]

    def finish(q):
        @pl.when(q == CHUNKS - 1)
        def _():
            @pl.when(root != mr)
            def _():
                left_copy(0).wait_recv()

        def arrived(t):
            block = lax.rem(mc + t, ncol)

            @pl.when(jnp.logical_or(
                jnp.logical_and(block < mc, mc + 1 >= ncol),
                jnp.logical_and(block > mc, mc <= 0),
            ))
            def _():
                piece(block, q, usend, mc).wait_recv()

        loop(1, ncol, arrived)

        @pl.when(jnp.logical_and(root == mr, slab_off // chunk == q))
        def _():
            left[...] = raw[:, pl.ds(slab_off, slab_count)]
            loop(1, nrow, lambda t: left_copy(t).start())

        @pl.when(q == CHUNKS - 1)
        def _():
            lr_ref[:slab_count, :] = dot(linv[...], left[...]).T

        at = pl.ds(pl.multiple_of(q * chunk, chunk), chunk)
        pt_ref[:, at] = dot(linv[...], raw[:, at])

    loop(0, CHUNKS, finish)

    loop(1, ncol, lambda t: diag_col(t, mc).wait_send())
    loop(1, nrow, lambda t: diag_row(t, mr).wait_send())
    loop(1, nrow, lambda t: rhs_copy(t, mr).wait_send())

    @pl.when(root == mr)
    def _():
        loop(1, nrow, lambda t: left_copy(t).wait_send())

    def sent(block):
        def chunk_sent(q):
            @pl.when(jnp.logical_and(block <= mc, mc + 1 < ncol))
            def _():
                piece(block, q, usend, mc + 1).wait_send()

            @pl.when(jnp.logical_and(block >= mc, mc > 0))
            def _():
                piece(block, q, wsend, mc - 1).wait_send()

        loop(0, CHUNKS, chunk_sent)

    loop(0, ncol, sent)


def update_kernel(w, slab_count, pt_ref, lr_ref, rs_ref, slab_ref, low_ref,
                  pf_ref, su_ref, rso_ref, ru_ref):
    mc = lax.axis_index("col")
    prod = dot(lr_ref[...], pt_ref[...])
    su_ref[...] = slab_ref[...] - prod[:slab_count]
    ru_ref[...] = low_ref[...] - prod[slab_count:]
    pf_ref[...] = pt_ref[pl.ds(pl.multiple_of(mc * w, w), w), :]
    rso_ref[...] = rs_ref[...]


def local(ncol, nrow, diag_block, panel_low, slab_rows, rhs_top, rhs_low):
    dr, dc = diag_block.shape
    rows, w = panel_low.shape
    nb = w * ncol
    slab_count = slab_rows.shape[0]
    nrhs, rk = rhs_top.shape
    pack = 128 // dc
    if dr % (8 * pack):
        pack = 1
    f32 = jnp.float32
    vm = pl.BlockSpec(memory_space=pltpu.VMEM)
    dma = pltpu.SemaphoreType.DMA
    pt, lr, rs = pl.pallas_call(
        functools.partial(gather_kernel, ncol, nrow, pack, slab_count),
        out_shape=(
            jax.ShapeDtypeStruct((nb, rows), f32),
            jax.ShapeDtypeStruct((slab_count + nrhs, nb), f32),
            jax.ShapeDtypeStruct((nrhs, rk), f32),
        ),
        in_specs=[pl.BlockSpec(memory_space=pl.ANY)] * 3,
        out_specs=(vm,) * 3,
        scratch_shapes=[
            pltpu.VMEM((dr, dc), f32),
            pltpu.VMEM((nrow, ncol, dr // pack, dc * pack), f32),
            pltpu.VMEM((nb, rows), f32),
            pltpu.VMEM((nb, slab_count), f32),
            pltpu.VMEM((nrow, nrhs, rk), f32),
            pltpu.VMEM((nb, 2 * nb), f32),
            pltpu.VMEM((nb, nb), f32),
            dma((3,)),
            dma((ncol,)), dma((ncol,)),
            dma((nrow,)), dma((nrow,)),
            dma((nrow,)), dma((nrow,)),
            dma((nrow,)), dma,
            dma((ncol, CHUNKS)), dma((ncol, CHUNKS)), dma((ncol, CHUNKS)),
        ],
        compiler_params=pltpu.CompilerParams(
            collective_id=0, has_side_effects=True, vmem_limit_bytes=40 * 1024 * 1024
        ),
    )(diag_block, panel_low.T, rhs_top)
    tile = rows // 4
    pf, su, rso, ru = pl.pallas_call(
        functools.partial(update_kernel, w, slab_count),
        grid=(4,),
        out_shape=(
            jax.ShapeDtypeStruct((w, rows), f32),
            jax.ShapeDtypeStruct(slab_rows.shape, f32),
            jax.ShapeDtypeStruct((nrhs, rk), f32),
            jax.ShapeDtypeStruct(rhs_low.shape, f32),
        ),
        in_specs=[
            pl.BlockSpec((nb, tile), lambda i: (0, i)),
            pl.BlockSpec((slab_count + nrhs, nb), lambda i: (0, 0)),
            pl.BlockSpec((nrhs, rk), lambda i: (0, 0)),
            pl.BlockSpec((slab_count, tile), lambda i: (0, i)),
            pl.BlockSpec((nrhs, tile), lambda i: (0, i)),
        ],
        out_specs=(
            pl.BlockSpec((w, tile), lambda i: (0, i)),
            pl.BlockSpec((slab_count, tile), lambda i: (0, i)),
            pl.BlockSpec((nrhs, rk), lambda i: (0, 0)),
            pl.BlockSpec((nrhs, tile), lambda i: (0, i)),
        ),
        compiler_params=pltpu.CompilerParams(vmem_limit_bytes=32 * 1024 * 1024),
    )(pt, lr, rs, slab_rows, rhs_low)
    return pf.T, su, rso, ru


def solution(mesh):
    ncol, nrow = mesh.shape["col"], mesh.shape["row"]
    return jax.shard_map(
        functools.partial(local, ncol, nrow),
        mesh=mesh,
        in_specs=(
            P("row", "col"),
            P(("groups", "row"), "col"),
            P("col", ("groups", "row")),
            P(("groups", "col"), "row"),
            P("col", ("groups", "row")),
        ),
        out_specs=(
            P(("groups", "row"), "col"),
            P("col", ("groups", "row")),
            P(("groups", "col"), "row"),
            P("col", ("groups", "row")),
        ),
        check_vma=False,
    )
```

```python
import functools

import jax
import jax.numpy as jnp
from jax import lax
from jax.experimental import pallas as pl
from jax.experimental.pallas import tpu as pltpu
from jax.sharding import PartitionSpec as P

MESH = pl.DeviceIdType.MESH
BS = 64
CHUNKS = 4
PIVOTS = 8
HIGH = lax.Precision.HIGHEST


def dot(a, b, contract=((1,), (0,))):
    return lax.dot_general(
        a, b, (contract, ((), ())), precision=HIGH, preferred_element_type=jnp.float32
    )


def eliminate(block):
    shape = (8, 2 * BS)
    row = lax.broadcasted_iota(jnp.int32, (BS, BS), 0)
    lane = lax.broadcasted_iota(jnp.int32, (BS, BS), 1)
    eye = jnp.where(row == lane, 1.0, 0.0).astype(jnp.float32)
    y = jnp.concatenate([block, eye], axis=1)
    groups = [y[g * 8 : g * 8 + 8] for g in range(BS // 8)]
    sub = lax.broadcasted_iota(jnp.int32, shape, 0)

    def wide(v):
        return jnp.broadcast_to(v, shape)

    for k in range(0, BS, PIVOTS):
        g0, s0 = k // 8, k % 8
        cols = [
            {g: wide(groups[g][:, k + j : k + j + 1]) for g in range(g0, BS // 8)}
            for j in range(PIVOTS)
        ]
        rows = [wide(groups[g0][s0 + j : s0 + j + 1, :]) for j in range(PIVOTS)]
        d = [
            [wide(cols[j][g0][s0 + i : s0 + i + 1, :]) for j in range(i + 1)]
            for i in range(PIVOTS)
        ]
        for j in range(PIVOTS):
            scale = lax.rsqrt(d[j][j])
            for i in range(j + 1, PIVOTS):
                d[i][j] = d[i][j] * scale
            for i in range(j + 1, PIVOTS):
                for m in range(j + 1, i + 1):
                    d[i][m] = d[i][m] - d[i][j] * d[m][j]
            rows[j] = rows[j] * scale
            for i in range(j + 1, PIVOTS):
                rows[i] = rows[i] - d[i][j] * rows[j]
            for g in cols[j]:
                cols[j][g] = cols[j][g] * scale
                for i in range(j + 1, PIVOTS):
                    cols[i][g] = cols[i][g] - cols[j][g] * d[i][j]
        for g in range(g0, BS // 8):
            if g == g0 and s0 + PIVOTS == 8:
                new = groups[g]
            else:
                new = groups[g]
                for j in range(PIVOTS):
                    new = new - cols[j][g] * rows[j]
            if g == g0:
                new = jnp.where(sub < s0, groups[g], new)
                for j in range(PIVOTS):
                    new = jnp.where(sub == s0 + j, rows[j], new)
            groups[g] = new
    return jnp.concatenate(groups, axis=0)[:, BS:]


def gather_kernel(
    ncol, nrow, pack, slab_count,
    diag_ref, panel_ref, rhs_ref, slab_ref, low_ref,
    pf_out, su_out, rs_out, ru_out,
    pf_ref, su_ref, rs_ref, ru_ref,
    pt_ref, lr_ref, dmine, dslots, raw, left, rslots, aug, linv,
    local_sem, d1send, d1recv, d2send, d2recv, rsend, rrecv,
    lsend, lrecv, usend, wsend, precv, osem,
):
    mc = lax.axis_index("col")
    mr = lax.axis_index("row")
    dr, dc = diag_ref.shape
    w, rows = panel_ref.shape
    nb = w * ncol
    chunk = rows // CHUNKS
    rk = rhs_ref.shape[1]

    def loop(lo, hi, body):
        def run(i, carry):
            body(i)
            return carry

        lax.fori_loop(lo, hi, run, 0)

    def on_col(t):
        return {"col": lax.rem(mc + t, ncol), "row": mr}

    def on_row(t):
        return {"col": mc, "row": lax.rem(mr + t, nrow)}

    def remote(src, dst, send, recv, to):
        return pltpu.make_async_remote_copy(
            src, dst, send, recv, device_id=to, device_id_type=MESH
        )

    barrier = pltpu.get_barrier_semaphore()
    loop(1, ncol, lambda t: pl.semaphore_signal(
        barrier, inc=1, device_id=on_col(t), device_id_type=MESH))
    loop(1, nrow, lambda t: pl.semaphore_signal(
        barrier, inc=1, device_id=on_row(t), device_id_type=MESH))

    mine = pl.ds(pl.multiple_of(mc * w, w), w)
    loads = (
        pltpu.make_async_copy(diag_ref, dmine, local_sem.at[0]),
        pltpu.make_async_copy(panel_ref, raw.at[mine, :], local_sem.at[1]),
        pltpu.make_async_copy(rhs_ref, rslots.at[mr], local_sem.at[2]),
        pltpu.make_async_copy(slab_ref, su_ref, local_sem.at[3]),
        pltpu.make_async_copy(low_ref, ru_ref, local_sem.at[4]),
    )
    for load in loads:
        load.start()
    loads[0].wait()
    x = dmine[...]
    step = dr // pack
    dslots[mr, mc] = jnp.concatenate([x[i * step : (i + 1) * step] for i in range(pack)], axis=1)
    loads[1].wait()
    loads[2].wait()
    slab_first = mc * slab_count
    root = slab_first // rows
    slab_off = pl.multiple_of(lax.rem(slab_first, rows), slab_count)

    pl.semaphore_wait(barrier, ncol + nrow - 2)

    def diag_col(t, slot):
        at = dslots.at[mr, slot]
        return remote(at, at, d1send.at[t], d1recv.at[slot], on_col(t))

    def diag_row(t, slot):
        at = dslots.at[slot]
        return remote(at, at, d2send.at[t], d2recv.at[slot], on_row(t))

    def rhs_copy(t, slot):
        at = rslots.at[slot]
        return remote(at, at, rsend.at[t], rrecv.at[slot], on_row(t))

    def left_copy(t):
        return remote(left, left, lsend.at[t], lrecv, on_row(t))

    def piece(block, q, sends, to):
        part = raw.at[
            pl.ds(pl.multiple_of(block * w, w), w),
            pl.ds(pl.multiple_of(q * chunk, chunk), chunk),
        ]
        return remote(part, part, sends.at[block, q], precv.at[block, q], {"col": to, "row": mr})

    loop(1, ncol, lambda t: diag_col(t, mc).start())

    def send_own(q):
        @pl.when(mc + 1 < ncol)
        def _():
            piece(mc, q, usend, mc + 1).start()

        @pl.when(mc > 0)
        def _():
            piece(mc, q, wsend, mc - 1).start()

    loop(0, CHUNKS, send_own)

    loop(1, ncol, lambda t: diag_col(t, lax.rem(mc + t, ncol)).wait_recv())
    loop(1, nrow, lambda t: diag_row(t, mr).start())
    loop(1, nrow, lambda t: rhs_copy(t, mr).start())

    def forward(e):
        s = e // CHUNKS + 1
        q = lax.rem(e, CHUNKS)

        @pl.when(jnp.logical_and(mc - s >= 0, mc + 1 < ncol))
        def _():
            piece(mc - s, q, usend, mc + 1).wait_recv()
            piece(mc - s, q, usend, mc + 1).start()

        @pl.when(jnp.logical_and(mc + s < ncol, mc > 0))
        def _():
            piece(mc + s, q, wsend, mc - 1).wait_recv()
            piece(mc + s, q, wsend, mc - 1).start()

    events = max(ncol - 2, 0) * CHUNKS
    early = events // 2
    each = -(-early // (nb // BS))

    ri = lax.broadcasted_iota(jnp.int32, (nb, nb), 0)
    ci = lax.broadcasted_iota(jnp.int32, (nb, nb), 1)
    aug[:, nb:] = jnp.where(ri == ci, 1.0, 0.0).astype(jnp.float32)
    loop(1, nrow, lambda t: diag_row(t, lax.rem(mr + t, nrow)).wait_recv())
    for r in range(nrow):
        parts = []
        for c in range(ncol):
            v = dslots[r, c]
            parts.append(
                jnp.concatenate([v[:, i * dc : (i + 1) * dc] for i in range(pack)], axis=0)
            )
        aug[r * dr : (r + 1) * dr, :nb] = jnp.concatenate(parts, axis=1)

    def block_step(b):
        loop(jnp.minimum(b * each, early), jnp.minimum((b + 1) * each, early), forward)
        here = pl.ds(pl.multiple_of(b * BS, BS), BS)
        panel = aug[here, :]
        rolled = pltpu.roll(panel[:, :nb], lax.rem(nb - b * BS, nb), 1)
        winv = eliminate(rolled[:, :BS])
        upper = dot(winv, panel)
        linv[here, :] = upper[:, nb:]

        @pl.when(b + 1 < nb // BS)
        def _():
            lane = lax.broadcasted_iota(jnp.int32, (BS, nb), 1)
            later = jnp.where(lane >= (b + 1) * BS, upper[:, :nb], 0.0)
            aug[...] = aug[...] - dot(later, upper, ((0,), (0,)))

    loop(0, nb // BS, block_step)
    loop(early, events, forward)

    loop(1, nrow, lambda t: rhs_copy(t, lax.rem(mr + t, nrow)).wait_recv())
    top = jnp.concatenate([rslots[r].T for r in range(nrow)], axis=0)
    rt = dot(linv[...], top).T
    lr_ref[slab_count:, :] = rt
    rs_ref[...] = pltpu.roll(rt, lax.rem(nb - mr * rk, nb), 1)[:, :rk]
    rs_write = pltpu.make_async_copy(rs_ref, rs_out, local_sem.at[5])
    rs_write.start()

    loads[3].wait()
    loads[4].wait()

    def writes(q):
        at = pl.ds(pl.multiple_of(q * chunk, chunk), chunk)
        return [
            pltpu.make_async_copy(here.at[:, at], there.at[:, at], osem.at[i, q])
            for i, (here, there) in enumerate(
                ((pf_ref, pf_out), (su_ref, su_out), (ru_ref, ru_out))
            )
        ]

    def update(q):
        at = pl.ds(pl.multiple_of(q * chunk, chunk), chunk)
        prod = dot(lr_ref[...], pt_ref[:, at])
        su_ref[:, at] = su_ref[:, at] - prod[:slab_count]
        ru_ref[:, at] = ru_ref[:, at] - prod[slab_count:]
        for write in writes(q):
            write.start()

    def finish(q):
        @pl.when(jnp.logical_and(q == CHUNKS - 1, root != mr))
        def _():
            left_copy(0).wait_recv()
            lr_ref[:slab_count, :] = dot(linv[...], left[...]).T
            loop(0, CHUNKS - 1, update)

        def arrived(t):
            block = lax.rem(mc + t, ncol)

            @pl.when(jnp.logical_or(
                jnp.logical_and(block < mc, mc + 1 >= ncol),
                jnp.logical_and(block > mc, mc <= 0),
            ))
            def _():
                piece(block, q, usend, mc).wait_recv()

        loop(1, ncol, arrived)

        @pl.when(jnp.logical_and(root == mr, slab_off // chunk == q))
        def _():
            left[...] = raw[:, pl.ds(slab_off, slab_count)]
            loop(1, nrow, lambda t: left_copy(t).start())
            lr_ref[:slab_count, :] = dot(linv[...], left[...]).T
            loop(0, q, update)

        at = pl.ds(pl.multiple_of(q * chunk, chunk), chunk)
        pt_ref[:, at] = dot(linv[...], raw[:, at])
        pf_ref[:, at] = pt_ref[mine, at]

        @pl.when(jnp.logical_or(
            jnp.logical_and(root == mr, q >= slab_off // chunk), q == CHUNKS - 1
        ))
        def _():
            update(q)

    loop(0, CHUNKS, finish)

    rs_write.wait()

    def written(q):
        for write in writes(q):
            write.wait()

    loop(0, CHUNKS, written)

    loop(1, ncol, lambda t: diag_col(t, mc).wait_send())
    loop(1, nrow, lambda t: diag_row(t, mr).wait_send())
    loop(1, nrow, lambda t: rhs_copy(t, mr).wait_send())

    @pl.when(root == mr)
    def _():
        loop(1, nrow, lambda t: left_copy(t).wait_send())

    def sent(block):
        def chunk_sent(q):
            @pl.when(jnp.logical_and(block <= mc, mc + 1 < ncol))
            def _():
                piece(block, q, usend, mc + 1).wait_send()

            @pl.when(jnp.logical_and(block >= mc, mc > 0))
            def _():
                piece(block, q, wsend, mc - 1).wait_send()

        loop(0, CHUNKS, chunk_sent)

    loop(0, ncol, sent)


def write_kernel(count, *refs):
    ins, outs, held = refs[:count], refs[count : 2 * count], refs[2 * count : 3 * count]
    load_sem, store_sem = refs[3 * count :]
    loads, stores = [], []
    for src, dst, buf in zip(ins, outs, held):
        size = 32 if src.shape[0] % 32 == 0 else src.shape[0]
        for first in range(0, src.shape[0], size):
            at = pl.ds(first, size)
            i = len(loads)
            loads.append(pltpu.make_async_copy(src.at[at, :], buf.at[at, :], load_sem.at[i]))
            stores.append(pltpu.make_async_copy(buf.at[at, :], dst.at[at, :], store_sem.at[i]))
    for load in loads:
        load.start()
    for load, store in zip(loads, stores):
        load.wait()
        store.start()
    for store in stores:
        store.wait()


def local(ncol, nrow, diag_block, panel_low, slab_rows, rhs_top, rhs_low):
    dr, dc = diag_block.shape
    rows, w = panel_low.shape
    nb = w * ncol
    slab_count = slab_rows.shape[0]
    nrhs, rk = rhs_top.shape
    pack = 128 // dc
    if dr % (8 * pack):
        pack = 1
    f32 = jnp.float32
    hbm = pl.BlockSpec(memory_space=pltpu.HBM)
    dma = pltpu.SemaphoreType.DMA
    outs = (
        jax.ShapeDtypeStruct((w, rows), f32),
        jax.ShapeDtypeStruct(slab_rows.shape, f32),
        jax.ShapeDtypeStruct((nrhs, rk), f32),
        jax.ShapeDtypeStruct(rhs_low.shape, f32),
    )
    done = pl.pallas_call(
        functools.partial(gather_kernel, ncol, nrow, pack, slab_count),
        out_shape=outs,
        in_specs=[hbm] * 5,
        out_specs=(hbm,) * 4,
        scratch_shapes=[
            *(pltpu.VMEM(out.shape, f32) for out in outs),
            pltpu.VMEM((nb, rows), f32),
            pltpu.VMEM((slab_count + nrhs, nb), f32),
            pltpu.VMEM((dr, dc), f32),
            pltpu.VMEM((nrow, ncol, dr // pack, dc * pack), f32),
            pltpu.VMEM((nb, rows), f32),
            pltpu.VMEM((nb, slab_count), f32),
            pltpu.VMEM((nrow, nrhs, rk), f32),
            pltpu.VMEM((nb, 2 * nb), f32),
            pltpu.VMEM((nb, nb), f32),
            dma((6,)),
            dma((ncol,)), dma((ncol,)),
            dma((nrow,)), dma((nrow,)),
            dma((nrow,)), dma((nrow,)),
            dma((nrow,)), dma,
            dma((ncol, CHUNKS)), dma((ncol, CHUNKS)), dma((ncol, CHUNKS)),
            dma((3, CHUNKS)),
        ],
        compiler_params=pltpu.CompilerParams(
            collective_id=0, has_side_effects=True, vmem_limit_bytes=61 * 1024 * 1024
        ),
    )(diag_block, panel_low.T, rhs_top, slab_rows, rhs_low)
    pieces = sum(-(-out.shape[0] // 32) for out in outs)
    pf, su, rs, ru = pl.pallas_call(
        functools.partial(write_kernel, len(outs)),
        out_shape=outs,
        in_specs=[hbm] * 4,
        out_specs=(hbm,) * 4,
        scratch_shapes=[
            *(pltpu.VMEM(out.shape, f32) for out in outs),
            dma((pieces,)), dma((pieces,)),
        ],
        compiler_params=pltpu.CompilerParams(vmem_limit_bytes=61 * 1024 * 1024),
    )(*done)
    return pf.T, su, rs, ru


def solution(mesh):
    ncol, nrow = mesh.shape["col"], mesh.shape["row"]
    return jax.shard_map(
        functools.partial(local, ncol, nrow),
        mesh=mesh,
        in_specs=(
            P("row", "col"),
            P(("groups", "row"), "col"),
            P("col", ("groups", "row")),
            P(("groups", "col"), "row"),
            P("col", ("groups", "row")),
        ),
        out_specs=(
            P(("groups", "row"), "col"),
            P("col", ("groups", "row")),
            P(("groups", "col"), "row"),
            P("col", ("groups", "row")),
        ),
        check_vma=False,
    )
```

```python
import functools

import jax
import jax.numpy as jnp
from jax import lax
from jax.experimental import pallas as pl
from jax.experimental.pallas import tpu as pltpu
from jax.sharding import PartitionSpec as P

MESH = pl.DeviceIdType.MESH
BS = 64
CHUNKS = 8
PIVOTS = 8
HIGH = lax.Precision.HIGHEST


def dot(a, b, contract=((1,), (0,))):
    return lax.dot_general(
        a, b, (contract, ((), ())), precision=HIGH, preferred_element_type=jnp.float32
    )


def eliminate(block):
    shape = (8, 2 * BS)
    row = lax.broadcasted_iota(jnp.int32, (BS, BS), 0)
    lane = lax.broadcasted_iota(jnp.int32, (BS, BS), 1)
    eye = jnp.where(row == lane, 1.0, 0.0).astype(jnp.float32)
    y = jnp.concatenate([block, eye], axis=1)
    groups = [y[g * 8 : g * 8 + 8] for g in range(BS // 8)]
    sub = lax.broadcasted_iota(jnp.int32, shape, 0)

    def wide(v):
        return jnp.broadcast_to(v, shape)

    for k in range(0, BS, PIVOTS):
        g0, s0 = k // 8, k % 8
        cols = [
            {g: wide(groups[g][:, k + j : k + j + 1]) for g in range(g0, BS // 8)}
            for j in range(PIVOTS)
        ]
        rows = [wide(groups[g0][s0 + j : s0 + j + 1, :]) for j in range(PIVOTS)]
        d = [
            [wide(cols[j][g0][s0 + i : s0 + i + 1, :]) for j in range(i + 1)]
            for i in range(PIVOTS)
        ]
        for j in range(PIVOTS):
            scale = lax.rsqrt(d[j][j])
            for i in range(j + 1, PIVOTS):
                d[i][j] = d[i][j] * scale
            for i in range(j + 1, PIVOTS):
                for m in range(j + 1, i + 1):
                    d[i][m] = d[i][m] - d[i][j] * d[m][j]
            rows[j] = rows[j] * scale
            for i in range(j + 1, PIVOTS):
                rows[i] = rows[i] - d[i][j] * rows[j]
            for g in cols[j]:
                cols[j][g] = cols[j][g] * scale
                for i in range(j + 1, PIVOTS):
                    cols[i][g] = cols[i][g] - cols[j][g] * d[i][j]
        for g in range(g0, BS // 8):
            if g == g0 and s0 + PIVOTS == 8:
                new = groups[g]
            else:
                new = groups[g]
                for j in range(PIVOTS):
                    new = new - cols[j][g] * rows[j]
            if g == g0:
                new = jnp.where(sub < s0, groups[g], new)
                for j in range(PIVOTS):
                    new = jnp.where(sub == s0 + j, rows[j], new)
            groups[g] = new
    return jnp.concatenate(groups, axis=0)[:, BS:]


def gather_kernel(
    ncol, nrow, pack, slab_count,
    diag_ref, panel_ref, rhs_ref, slab_ref, low_ref,
    pf_out, su_out, rs_out, ru_out,
    pf_ref, su_ref, rs_ref, ru_ref,
    pt_ref, lr_ref, dmine, dslots, raw, left, rslots, aug, linv,
    local_sem, d1send, d1recv, d2send, d2recv, rsend, rrecv,
    lsend, lrecv, usend, wsend, precv, osem,
):
    mc = lax.axis_index("col")
    mr = lax.axis_index("row")
    dr, dc = diag_ref.shape
    w, rows = panel_ref.shape
    nb = w * ncol
    chunk = rows // CHUNKS
    rk = rhs_ref.shape[1]

    def loop(lo, hi, body):
        def run(i, carry):
            body(i)
            return carry

        lax.fori_loop(lo, hi, run, 0)

    def on_col(t):
        return {"col": lax.rem(mc + t, ncol), "row": mr}

    def on_row(t):
        return {"col": mc, "row": lax.rem(mr + t, nrow)}

    def remote(src, dst, send, recv, to):
        return pltpu.make_async_remote_copy(
            src, dst, send, recv, device_id=to, device_id_type=MESH
        )

    barrier = pltpu.get_barrier_semaphore()
    loop(1, ncol, lambda t: pl.semaphore_signal(
        barrier, inc=1, device_id=on_col(t), device_id_type=MESH))
    loop(1, nrow, lambda t: pl.semaphore_signal(
        barrier, inc=1, device_id=on_row(t), device_id_type=MESH))

    mine = pl.ds(pl.multiple_of(mc * w, w), w)
    loads = (
        pltpu.make_async_copy(diag_ref, dmine, local_sem.at[0]),
        pltpu.make_async_copy(panel_ref, raw.at[mine, :], local_sem.at[1]),
        pltpu.make_async_copy(rhs_ref, rslots.at[mr], local_sem.at[2]),
        pltpu.make_async_copy(slab_ref, su_ref, local_sem.at[3]),
        pltpu.make_async_copy(low_ref, ru_ref, local_sem.at[4]),
    )
    for load in loads:
        load.start()
    loads[0].wait()
    x = dmine[...]
    step = dr // pack
    dslots[mr, mc] = jnp.concatenate([x[i * step : (i + 1) * step] for i in range(pack)], axis=1)
    loads[1].wait()
    loads[2].wait()
    slab_first = mc * slab_count
    root = slab_first // rows
    slab_off = pl.multiple_of(lax.rem(slab_first, rows), slab_count)

    pl.semaphore_wait(barrier, ncol + nrow - 2)

    def diag_col(t, slot):
        at = dslots.at[mr, slot]
        return remote(at, at, d1send.at[t], d1recv.at[slot], on_col(t))

    def diag_row(t, slot):
        at = dslots.at[slot]
        return remote(at, at, d2send.at[t], d2recv.at[slot], on_row(t))

    def rhs_copy(t, slot):
        at = rslots.at[slot]
        return remote(at, at, rsend.at[t], rrecv.at[slot], on_row(t))

    def left_copy(t):
        return remote(left, left, lsend.at[t], lrecv, on_row(t))

    def piece(block, q, sends, to):
        part = raw.at[
            pl.ds(pl.multiple_of(block * w, w), w),
            pl.ds(pl.multiple_of(q * chunk, chunk), chunk),
        ]
        return remote(part, part, sends.at[block, q], precv.at[block, q], {"col": to, "row": mr})

    loop(1, ncol, lambda t: diag_col(t, mc).start())

    def send_own(q):
        @pl.when(mc + 1 < ncol)
        def _():
            piece(mc, q, usend, mc + 1).start()

        @pl.when(mc > 0)
        def _():
            piece(mc, q, wsend, mc - 1).start()

    loop(0, CHUNKS, send_own)

    loop(1, ncol, lambda t: diag_col(t, lax.rem(mc + t, ncol)).wait_recv())
    loop(1, nrow, lambda t: diag_row(t, mr).start())
    loop(1, nrow, lambda t: rhs_copy(t, mr).start())

    def forward(e):
        s = e // CHUNKS + 1
        q = lax.rem(e, CHUNKS)

        @pl.when(jnp.logical_and(mc - s >= 0, mc + 1 < ncol))
        def _():
            piece(mc - s, q, usend, mc + 1).wait_recv()
            piece(mc - s, q, usend, mc + 1).start()

        @pl.when(jnp.logical_and(mc + s < ncol, mc > 0))
        def _():
            piece(mc + s, q, wsend, mc - 1).wait_recv()
            piece(mc + s, q, wsend, mc - 1).start()

    events = max(ncol - 2, 0) * CHUNKS
    early = events // 2
    each = -(-early // (nb // BS))

    ri = lax.broadcasted_iota(jnp.int32, (nb, nb), 0)
    ci = lax.broadcasted_iota(jnp.int32, (nb, nb), 1)
    aug[:, nb:] = jnp.where(ri == ci, 1.0, 0.0).astype(jnp.float32)
    loop(1, nrow, lambda t: diag_row(t, lax.rem(mr + t, nrow)).wait_recv())
    for r in range(nrow):
        parts = []
        for c in range(ncol):
            v = dslots[r, c]
            parts.append(
                jnp.concatenate([v[:, i * dc : (i + 1) * dc] for i in range(pack)], axis=0)
            )
        aug[r * dr : (r + 1) * dr, :nb] = jnp.concatenate(parts, axis=1)

    def block_step(b):
        loop(jnp.minimum(b * each, early), jnp.minimum((b + 1) * each, early), forward)
        here = pl.ds(pl.multiple_of(b * BS, BS), BS)
        panel = aug[here, :]
        rolled = pltpu.roll(panel[:, :nb], lax.rem(nb - b * BS, nb), 1)
        winv = eliminate(rolled[:, :BS])
        upper = dot(winv, panel)
        linv[here, :] = upper[:, nb:]

        @pl.when(b + 1 < nb // BS)
        def _():
            lane = lax.broadcasted_iota(jnp.int32, (BS, nb), 1)
            later = jnp.where(lane >= (b + 1) * BS, upper[:, :nb], 0.0)
            aug[...] = aug[...] - dot(later, upper, ((0,), (0,)))

    loop(0, nb // BS, block_step)
    loop(early, events, forward)

    loop(1, nrow, lambda t: rhs_copy(t, lax.rem(mr + t, nrow)).wait_recv())
    top = jnp.concatenate([rslots[r].T for r in range(nrow)], axis=0)
    rt = dot(linv[...], top).T
    lr_ref[slab_count:, :] = rt
    rs_ref[...] = pltpu.roll(rt, lax.rem(nb - mr * rk, nb), 1)[:, :rk]
    rs_write = pltpu.make_async_copy(rs_ref, rs_out, local_sem.at[5])
    rs_write.start()

    loads[3].wait()
    loads[4].wait()

    def writes(q):
        at = pl.ds(pl.multiple_of(q * chunk, chunk), chunk)
        return [
            pltpu.make_async_copy(here.at[:, at], there.at[:, at], osem.at[i, q])
            for i, (here, there) in enumerate(
                ((pf_ref, pf_out), (su_ref, su_out), (ru_ref, ru_out))
            )
        ]

    def update(q):
        at = pl.ds(pl.multiple_of(q * chunk, chunk), chunk)
        prod = dot(lr_ref[...], pt_ref[:, at])
        su_ref[:, at] = su_ref[:, at] - prod[:slab_count]
        ru_ref[:, at] = ru_ref[:, at] - prod[slab_count:]
        for write in writes(q):
            write.start()

    def finish(q):
        @pl.when(jnp.logical_and(q == CHUNKS - 1, root != mr))
        def _():
            left_copy(0).wait_recv()
            lr_ref[:slab_count, :] = dot(linv[...], left[...]).T
            loop(0, CHUNKS - 1, update)

        def arrived(t):
            block = lax.rem(mc + t, ncol)

            @pl.when(jnp.logical_or(
                jnp.logical_and(block < mc, mc + 1 >= ncol),
                jnp.logical_and(block > mc, mc <= 0),
            ))
            def _():
                piece(block, q, usend, mc).wait_recv()

        loop(1, ncol, arrived)

        @pl.when(jnp.logical_and(root == mr, slab_off // chunk == q))
        def _():
            left[...] = raw[:, pl.ds(slab_off, slab_count)]
            loop(1, nrow, lambda t: left_copy(t).start())
            lr_ref[:slab_count, :] = dot(linv[...], left[...]).T
            loop(0, q, update)

        at = pl.ds(pl.multiple_of(q * chunk, chunk), chunk)
        pt_ref[:, at] = dot(linv[...], raw[:, at])
        pf_ref[:, at] = pt_ref[mine, at]

        @pl.when(jnp.logical_or(
            jnp.logical_and(root == mr, q >= slab_off // chunk), q == CHUNKS - 1
        ))
        def _():
            update(q)

    loop(0, CHUNKS, finish)

    rs_write.wait()

    def written(q):
        for write in writes(q):
            write.wait()

    loop(0, CHUNKS, written)

    loop(1, ncol, lambda t: diag_col(t, mc).wait_send())
    loop(1, nrow, lambda t: diag_row(t, mr).wait_send())
    loop(1, nrow, lambda t: rhs_copy(t, mr).wait_send())

    @pl.when(root == mr)
    def _():
        loop(1, nrow, lambda t: left_copy(t).wait_send())

    def sent(block):
        def chunk_sent(q):
            @pl.when(jnp.logical_and(block <= mc, mc + 1 < ncol))
            def _():
                piece(block, q, usend, mc + 1).wait_send()

            @pl.when(jnp.logical_and(block >= mc, mc > 0))
            def _():
                piece(block, q, wsend, mc - 1).wait_send()

        loop(0, CHUNKS, chunk_sent)

    loop(0, ncol, sent)


def write_kernel(count, *refs):
    ins, outs, held = refs[:count], refs[count : 2 * count], refs[2 * count : 3 * count]
    load_sem, store_sem = refs[3 * count :]
    loads, stores = [], []
    for src, dst, buf in zip(ins, outs, held):
        size = 32 if src.shape[0] % 32 == 0 else src.shape[0]
        for first in range(0, src.shape[0], size):
            at = pl.ds(first, size)
            i = len(loads)
            loads.append(pltpu.make_async_copy(src.at[at, :], buf.at[at, :], load_sem.at[i]))
            stores.append(pltpu.make_async_copy(buf.at[at, :], dst.at[at, :], store_sem.at[i]))
    for load in loads:
        load.start()
    for load, store in zip(loads, stores):
        load.wait()
        store.start()
    for store in stores:
        store.wait()


def local(ncol, nrow, diag_block, panel_low, slab_rows, rhs_top, rhs_low):
    dr, dc = diag_block.shape
    rows, w = panel_low.shape
    nb = w * ncol
    slab_count = slab_rows.shape[0]
    nrhs, rk = rhs_top.shape
    pack = 128 // dc
    if dr % (8 * pack):
        pack = 1
    f32 = jnp.float32
    hbm = pl.BlockSpec(memory_space=pltpu.HBM)
    dma = pltpu.SemaphoreType.DMA
    outs = (
        jax.ShapeDtypeStruct((w, rows), f32),
        jax.ShapeDtypeStruct(slab_rows.shape, f32),
        jax.ShapeDtypeStruct((nrhs, rk), f32),
        jax.ShapeDtypeStruct(rhs_low.shape, f32),
    )
    done = pl.pallas_call(
        functools.partial(gather_kernel, ncol, nrow, pack, slab_count),
        out_shape=outs,
        in_specs=[hbm] * 5,
        out_specs=(hbm,) * 4,
        scratch_shapes=[
            *(pltpu.VMEM(out.shape, f32) for out in outs),
            pltpu.VMEM((nb, rows), f32),
            pltpu.VMEM((slab_count + nrhs, nb), f32),
            pltpu.VMEM((dr, dc), f32),
            pltpu.VMEM((nrow, ncol, dr // pack, dc * pack), f32),
            pltpu.VMEM((nb, rows), f32),
            pltpu.VMEM((nb, slab_count), f32),
            pltpu.VMEM((nrow, nrhs, rk), f32),
            pltpu.VMEM((nb, 2 * nb), f32),
            pltpu.VMEM((nb, nb), f32),
            dma((6,)),
            dma((ncol,)), dma((ncol,)),
            dma((nrow,)), dma((nrow,)),
            dma((nrow,)), dma((nrow,)),
            dma((nrow,)), dma,
            dma((ncol, CHUNKS)), dma((ncol, CHUNKS)), dma((ncol, CHUNKS)),
            dma((3, CHUNKS)),
        ],
        compiler_params=pltpu.CompilerParams(
            collective_id=0, has_side_effects=True, vmem_limit_bytes=61 * 1024 * 1024
        ),
    )(diag_block, panel_low.T, rhs_top, slab_rows, rhs_low)
    pieces = sum(-(-out.shape[0] // 32) for out in outs)
    pf, su, rs, ru = pl.pallas_call(
        functools.partial(write_kernel, len(outs)),
        out_shape=outs,
        in_specs=[hbm] * 4,
        out_specs=(hbm,) * 4,
        scratch_shapes=[
            *(pltpu.VMEM(out.shape, f32) for out in outs),
            dma((pieces,)), dma((pieces,)),
        ],
        compiler_params=pltpu.CompilerParams(vmem_limit_bytes=61 * 1024 * 1024),
    )(*done)
    return pf.T, su, rs, ru


def solution(mesh):
    ncol, nrow = mesh.shape["col"], mesh.shape["row"]
    return jax.shard_map(
        functools.partial(local, ncol, nrow),
        mesh=mesh,
        in_specs=(
            P("row", "col"),
            P(("groups", "row"), "col"),
            P("col", ("groups", "row")),
            P(("groups", "col"), "row"),
            P("col", ("groups", "row")),
        ),
        out_specs=(
            P(("groups", "row"), "col"),
            P("col", ("groups", "row")),
            P(("groups", "col"), "row"),
            P("col", ("groups", "row")),
        ),
        check_vma=False,
    )
```
